32 devices in a mesh: dp: 8 (over z, y), row: 2 (over core), col: 2 (over x).
Axes of the slice: x: 2, y: 2, z: 4, core: 2. Of those that a mesh axis runs over, the one named last changes fastest.
Arguments:
- tokens: bfloat16 [8192, 1024], P('dp', ('row', 'col')), may hold values from -6 to 6
- lengths: int32 [8, 3], P('dp'), may hold values from 1 to 512, 1024 in all within a row
- ln1_gain: float32 [1024], P(('row', 'col')), may hold values from 0.25 to 1.75
- ln1_shift: float32 [1024], P(('row', 'col')), may hold values from -3 to 3
- w_qkv: bfloat16 [1024, 3072], P('row', 'col'), may hold values from -0.1875 to 0.1875
- b_qv: float32 [2048], P('col'), may hold values from -3 to 3
- w_out: bfloat16 [1024, 1024], P('col', 'row'), may hold values from -0.75 to 0.75
- b_out: float32 [1024], P(('row', 'col')), may hold values from -3 to 3
- ln2_gain: float32 [1024], P(('row', 'col')), may hold values from 0.25 to 1.75
- ln2_shift: float32 [1024], P(('row', 'col')), may hold values from -3 to 3
- w_up: bfloat16 [1024, 4096], P('row', 'col'), may hold values from -0.1875 to 0.1875
- b_up: float32 [4096], P('col'), may hold values from -3 to 3
- w_down: bfloat16 [4096, 1024], P('col', 'row'), may hold values from -0.09375 to 0.09375
- b_down: float32 [1024], P(('row', 'col')), may hold values from -3 to 3
- cotangent: bfloat16 [8192, 1024], P('dp', ('row', 'col')), may hold values from -6 to 6
Outputs:
- block_out: bfloat16 [8192, 1024], P('dp', ('row', 'col'))
- grad_input: float32 [8192, 1024], P('dp', ('row', 'col'))
- grad_ln1_gain: float32 [1024], P(('row', 'col'))
- grad_ln1_shift: float32 [1024], P(('row', 'col'))
- grad_w_qkv: float32 [1024, 3072], P('row', 'col')
- grad_b_qv: float32 [2048], P('col')
- grad_w_out: float32 [1024, 1024], P('col', 'row')
- grad_b_out: float32 [1024], P(('row', 'col'))
- grad_ln2_gain: float32 [1024], P(('row', 'col'))
- grad_ln2_shift: float32 [1024], P(('row', 'col'))
- grad_w_up: float32 [1024, 4096], P('row', 'col')
- grad_b_up: float32 [4096], P('col')
- grad_w_down: float32 [4096, 1024], P('col', 'row')
- grad_b_down: float32 [1024], P(('row', 'col'))
The draws below stay inside these ranges and needn't reach their ends.
Inputs may be any that keep to these rules, and one draw needn't show every extreme that they name: Row g lists in order the lengths of the sequences packed into the 1024 tokens of data group g; each row sums to 1024 and its longest is exactly 512.
All inputs are finite; a program needn't handle non-finite values.
Results may differ from the reference program's by a relative error of at most 0.0093.
Values may be sent and summed in bfloat16 or wider, within the bound.
A program may use at most 128 MiB of HBM per device.

```python
import math
import jax
import jax.numpy as jnp
import numpy as np
from jax import lax

D = 1024
HEADS = 16
HEAD_DIM = 64
FF = 4096
TOK_DEV = 1024
MAXLEN = 512
SEQS = 3
QB = 512
KW = 1024
TOKENS = 8192
N_DP = 8


def shard_levels(rng, extent, split, smallest, high):
    def one(axis_at, parts):
        heights = jax.random.uniform(jax.random.fold_in(jax.random.fold_in(rng, 6), axis_at), (parts,), jnp.float32, smallest / len(split), high / len(split))
        return jnp.repeat(jnp.exp(heights), extent[axis_at] // parts).reshape((-1,) + (1,) * (len(extent) - axis_at - 1))

    level = one(*split[0])
    for cut in split[1:]:
        level = level * one(*cut)
    return level


def length_profile(amount, total, limit, skew):
    portions = [(1 << 20) // math.isqrt(grade ** skew) + 1 for grade in range(2, amount + 1)]
    surplus, holding = total - limit - (amount - 1), [1] * (amount - 1)
    while surplus > 0:
        movable = [i for i in range(amount - 1) if holding[i] < limit]
        pool, budget = sum([portions[i] for i in movable]), surplus
        for i in movable:
            more = min(limit - holding[i], max(1, budget * portions[i] // pool), surplus)
            holding[i] = holding[i] + more
            surplus = surplus - more
    return np.array([limit] + holding)


def ragged(stream_key, count, total, bound, skew):
    if count == 2:
        one = jax.random.randint(stream_key, (), max(1, total - bound), min(bound, total - 1) + 1)
        return jnp.stack([one, total - one])
    sizes = jnp.asarray(length_profile(count, total, bound, skew), jnp.int32)
    pairs = (count - 1) // 2
    source_of, sink = sizes[1:1 + 2 * pairs:2], sizes[2:2 + 2 * pairs:2]
    room = jnp.minimum(source_of - 1, bound - sink)
    moved = jax.random.randint(jax.random.fold_in(stream_key, 1), (pairs,), 0, 1 << 20) % (room + 1)
    sizes = sizes.at[1:1 + 2 * pairs:2].set(source_of - moved).at[2:2 + 2 * pairs:2].set(sink + moved)
    return sizes[jax.random.permutation(jax.random.fold_in(stream_key, 2), count)]


def gaussian(rng, shape, width, limit, split=(), held_as=jnp.bfloat16):
    values = width * jax.random.normal(rng, shape, jnp.float32)
    if split:
        values = values * shard_levels(rng, shape, split, -0.22, 0.18)
    return jnp.clip(values, -limit, limit).astype(held_as)


def setup_inputs(seed: int = 0) -> dict:
    keys = jax.random.split(jax.random.key(seed), 16)
    tokens = gaussian(keys[0], (TOKENS, D), 1.0, 6.0, ((0, 8), (1, 4)))
    lengths = jax.vmap(lambda own: ragged(own, SEQS, TOK_DEV, MAXLEN, 2))(jax.random.split(keys[1], N_DP)).reshape((N_DP, SEQS)).astype(jnp.int32)
    ln1_gain = jnp.clip(1.0 + 0.15 * jax.random.normal(keys[2], (D,), jnp.float32), 0.25, 1.75)
    ln1_shift = gaussian(keys[3], (D,), 0.3, 3.0, ((0, 4),), jnp.float32)
    w_qkv = gaussian(keys[4], (D, 3 * D), D ** -0.5, 0.1875, ((0, 2), (1, 2)))
    b_qv = gaussian(keys[5], (2 * D,), 0.5, 3.0, ((0, 2),), jnp.float32)
    w_out = gaussian(keys[6], (D, D), HEAD_DIM ** -0.5, 0.75, ((0, 2), (1, 2)))
    b_out = gaussian(keys[7], (D,), 0.5, 3.0, ((0, 4),), jnp.float32)
    ln2_gain = jnp.clip(1.0 + 0.15 * jax.random.normal(keys[8], (D,), jnp.float32), 0.25, 1.75)
    ln2_shift = gaussian(keys[9], (D,), 0.3, 3.0, ((0, 4),), jnp.float32)
    w_up = gaussian(keys[10], (D, FF), D ** -0.5, 0.1875, ((0, 2), (1, 2)))
    b_up = gaussian(keys[11], (FF,), 0.5, 3.0, ((0, 2),), jnp.float32)
    w_down = gaussian(keys[12], (FF, D), FF ** -0.5, 0.09375, ((0, 2), (1, 2)))
    b_down = gaussian(keys[13], (D,), 0.5, 3.0, ((0, 4),), jnp.float32)
    cotangent = gaussian(keys[14], (TOKENS, D), 1.0, 6.0, ((0, 8), (1, 4)))
    return dict(tokens=tokens, lengths=lengths, ln1_gain=ln1_gain, ln1_shift=ln1_shift, w_qkv=w_qkv, b_qv=b_qv, w_out=w_out, b_out=b_out, ln2_gain=ln2_gain, ln2_shift=ln2_shift, w_up=w_up, b_up=b_up, w_down=w_down, b_down=b_down, cotangent=cotangent)


EPSILON = 1e-05
HIGHEST = lax.Precision.HIGHEST

@jax.custom_vjp
def low(v):
    return lax.optimization_barrier(v.astype(jnp.bfloat16)).astype(jnp.float32)

@jax.custom_vjp
def low_back(v):
    return v

def low_keep(v):
    return (low(v), None)

def low_pass(kept, grad):
    return (grad,)

def back_keep(v):
    return (v, None)

def back_low(kept, grad):
    return (low(grad),)
low.defvjp(low_keep, low_pass)
low_back.defvjp(back_keep, back_low)

def layer_norm(values, gain, shift):
    center = lax.optimization_barrier(jnp.mean(values, axis=-1, keepdims=True))
    spread = lax.optimization_barrier(jnp.mean(values * values, axis=-1, keepdims=True)) - center * center
    return (values - center) * lax.rsqrt(spread + EPSILON) * gain + shift

def segment_ids(lengths, count):
    ends = jnp.cumsum(lengths.astype(jnp.int32)).astype(jnp.int32)
    places = jnp.arange(count, dtype=jnp.int32)
    return lax.optimization_barrier(jnp.sum((places[:, None] >= ends[None, :]).astype(jnp.int32), axis=1)).astype(jnp.int32)

def attention(queries, key_rows, value_rows, segment, slopes):
    row_count = queries.shape[0]
    scale = HEAD_DIM ** (-0.5)
    starts = jnp.arange(row_count // QB, dtype=jnp.int32) * QB

    def one_block(offset):
        key_first = jnp.clip(offset + QB - KW, 0, row_count - KW).astype(jnp.int32)
        query_block = lax.dynamic_slice_in_dim(queries, offset, QB, 0)
        key_block = lax.dynamic_slice_in_dim(key_rows, key_first, KW, 0)
        value_block = lax.dynamic_slice_in_dim(value_rows, key_first, KW, 0)
        query_place = offset + jnp.arange(QB, dtype=jnp.int32)
        key_place = key_first + jnp.arange(KW, dtype=jnp.int32)
        query_seg = lax.dynamic_slice_in_dim(segment, offset, QB, 0)
        key_seg = lax.dynamic_slice_in_dim(segment, key_first, KW, 0)
        allowed = (query_seg[:, None] == key_seg[None, :]) & (key_place[None, :] <= query_place[:, None])
        distance = (query_place[:, None] - key_place[None, :]).astype(jnp.float32)
        scores = jnp.einsum('qhd,khd->hqk', query_block, key_block, precision=HIGHEST) * scale
        scores = low_back(scores - slopes[:, None, None] * distance[None])
        scores = jnp.where(allowed[None], scores, -1000000000.0)
        ceiling = lax.optimization_barrier(jnp.max(scores, axis=-1, keepdims=True))
        weights = jnp.exp(scores - ceiling)
        weights = weights / lax.optimization_barrier(jnp.sum(weights, axis=-1, keepdims=True))
        return jnp.einsum('hqk,khd->qhd', low(weights), value_block, precision=HIGHEST)
    blocks = lax.map(jax.checkpoint(one_block), starts)
    return blocks.reshape(row_count, queries.shape[1], queries.shape[2])

def forward(inputs, ln1_gain, ln1_shift, w_qkv, b_qv, w_out, b_out, ln2_gain, ln2_shift, w_up, b_up, w_down, b_down, segment):
    row_count = inputs.shape[0]
    head_ids = jnp.arange(HEADS, dtype=jnp.float32)
    slopes = jnp.exp2(-8.0 * (head_ids + 1.0) / HEADS)
    normed1 = low(layer_norm(inputs, ln1_gain, ln1_shift))
    pair_bias = b_qv.reshape(HEADS, 2, HEAD_DIM)
    joined_bias = jnp.stack([pair_bias[:, 0], jnp.zeros_like(pair_bias[:, 0]), pair_bias[:, 1]], axis=1).reshape(3 * D)
    mixed = jnp.dot(normed1, w_qkv, precision=HIGHEST) + joined_bias
    mixed = low(low_back(mixed)).reshape(row_count, HEADS, 3, HEAD_DIM)
    context = attention(mixed[:, :, 0], mixed[:, :, 1], mixed[:, :, 2], segment, slopes).reshape(row_count, D)
    context = low(low_back(context))
    after = inputs + low_back(jnp.dot(context, w_out, precision=HIGHEST)) + b_out
    normed2 = low(layer_norm(after, ln2_gain, ln2_shift))
    preact = low_back(jnp.dot(normed2, w_up, precision=HIGHEST) + b_up)
    active = low(jax.nn.gelu(preact, approximate=True))
    return after + low_back(jnp.dot(active, w_down, precision=HIGHEST)) + b_down

def reference(tokens, lengths, ln1_gain, ln1_shift, w_qkv, b_qv, w_out, b_out, ln2_gain, ln2_shift, w_up, b_up, w_down, b_down, cotangent):
    params = tuple((p.astype(jnp.float32) for p in (ln1_gain, ln1_shift, w_qkv, b_qv, w_out, b_out, ln2_gain, ln2_shift, w_up, b_up, w_down, b_down)))

    def one_group(totals, items):
        group_rows, group_cot, group_lengths = items
        segment = segment_ids(group_lengths, group_rows.shape[0])

        def run_layer(inputs, *weights):
            return forward(inputs, *weights, segment)
        result, pull = jax.vjp(run_layer, group_rows.astype(jnp.float32), *params)
        grads = pull(group_cot.astype(jnp.float32))
        new_totals = tuple((a + b for a, b in zip(totals, grads[1:])))
        return (new_totals, (result.astype(jnp.bfloat16), grads[0]))
    initial = tuple((jnp.zeros_like(p) for p in params))
    totals, (outputs, grad_rows) = lax.scan(one_group, initial, (tokens.reshape(N_DP, TOK_DEV, D), cotangent.reshape(N_DP, TOK_DEV, D), lengths))
    return (outputs.reshape(TOKENS, D), grad_rows.reshape(TOKENS, D), totals[0], totals[1], totals[2], totals[3], totals[4], totals[5], totals[6], totals[7], totals[8], totals[9], totals[10], totals[11])
```

```python
import functools

import jax
import jax.numpy as jnp
from jax import lax
from jax.experimental import pallas as pl
from jax.experimental.pallas import tpu as pltpu
from jax.sharding import PartitionSpec as P

HEADS = 16
HEAD_DIM = 64
MAXLEN = 512
BLOCK = 256
PAIR = 6 * HEAD_DIM
EPSILON = 1e-05
FAR = 1e12
BF = jnp.bfloat16
F32 = jnp.float32


def swap_row(values):
    return lax.ppermute(values, "row", [(0, 1), (1, 0)])


def swap_col(values):
    return lax.ppermute(values, "col", [(0, 1), (1, 0)])


def ring_sum(values):
    size = lax.axis_size("dp")
    if size == 1:
        return values
    places = list(range(0, size, 2)) + list(range(size - 1, 0, -2))
    forward = [(places[i], places[(i + 1) % size]) for i in range(size)]
    backward = [(to, start) for start, to in forward]
    place = jnp.array([places.index(i) for i in range(size)], jnp.int32)[lax.axis_index("dp")]
    rows = values.shape[0] // (2 * size)
    result = jnp.zeros(values.shape, values.dtype)
    held = [None, None]
    for step in range(2 * size - 1):
        for way, (perm, sign) in enumerate(((forward, 1), (backward, -1))):
            chunk = (place - sign * step) % size
            offset = (way * size + chunk) * rows
            if step == 0:
                held[way] = lax.dynamic_slice_in_dim(values, offset, rows, 0)
                continue
            held[way] = lax.ppermute(held[way], "dp", perm)
            if step < size:
                held[way] = held[way] + lax.dynamic_slice_in_dim(values, offset, rows, 0)
            if step >= size - 1:
                result = lax.dynamic_update_slice_in_dim(result, held[way], offset, 0)
    return result


def small_sum(values):
    size = lax.axis_size("dp")
    if size & (size - 1):
        return lax.psum(values, "dp")
    bit = 1
    while bit < size:
        values = values + lax.ppermute(values, "dp", [(i, i ^ bit) for i in range(size)])
        bit *= 2
    return values


def nothing(values):
    return values[0, 0].astype(F32) * 0.0


def part(values, index, axis):
    width = values.shape[axis] // 2
    return lax.dynamic_slice_in_dim(values, index * width, width, axis)


def in_order(index, mine, theirs, axis):
    first = jnp.where(index == 0, mine, theirs)
    second = jnp.where(index == 0, theirs, mine)
    return jnp.concatenate([first, second], axis)


def dot(a, b):
    return lax.dot_general(a, b, (((1,), (0,)), ((), ())), preferred_element_type=F32)


def dot_nt(a, b):
    return lax.dot_general(a, b, (((1,), (1,)), ((), ())), preferred_element_type=F32)


def dot_tn(a, b):
    return lax.dot_general(a, b, (((0,), (0,)), ((), ())), preferred_element_type=F32)


def key_start(block):
    return max(0, block * BLOCK - -(-(MAXLEN - 1) // BLOCK) * BLOCK)


def masked_distance(seg_col, seg_row, block):
    low, high = key_start(block), (block + 1) * BLOCK
    rows = slice(block * BLOCK, high)
    query = block * BLOCK + lax.broadcasted_iota(jnp.int32, (BLOCK, high - low), 0)
    key = low + lax.broadcasted_iota(jnp.int32, (BLOCK, high - low), 1)
    allowed = (seg_col[rows, :] == seg_row[:, low:high]) & (key <= query)
    return jnp.where(allowed, (query - key).astype(F32), FAR)


def slope_of(head):
    return jnp.exp2(-8.0 * (jnp.full((1, 1), head, jnp.int32).astype(F32) + 1.0) / HEADS)


def first_head(step, heads):
    return (lax.axis_index("col") * 2 + lax.axis_index("row")) * heads + 2 * step


def forward_kernel(heads, mixed, seg_col, seg_row, context, logsum):
    base = first_head(pl.program_id(0), heads)
    for block in range(mixed.shape[0] // BLOCK):
        low, high = key_start(block), (block + 1) * BLOCK
        rows = slice(block * BLOCK, high)
        distance = masked_distance(seg_col, seg_row, block)
        outs, logs = [], []
        for head in range(2):
            at = head * 3 * HEAD_DIM
            query = mixed[rows, at : at + HEAD_DIM] * BF(HEAD_DIM**-0.5)
            keys = mixed[low:high, at + HEAD_DIM : at + 2 * HEAD_DIM]
            values = mixed[low:high, at + 2 * HEAD_DIM : at + 3 * HEAD_DIM]
            scores = dot_nt(query, keys) - slope_of(base + head) * distance
            ceiling = jnp.max(scores, axis=1, keepdims=True)
            weights = jnp.exp(scores - ceiling)
            total = jnp.sum(weights, axis=1, keepdims=True)
            outs.append(dot(weights.astype(BF), values) / total)
            logs.append(ceiling + jnp.log(total))
        context[rows, :] = jnp.concatenate(outs, 1).astype(BF)
        logsum[0, rows, :] = jnp.concatenate(logs, 1)


def backward_kernel(heads, mixed, seg_col, seg_row, logsum, grad_context, grad_mixed, sums):
    base = first_head(pl.program_id(0), heads)
    sums[...] = jnp.zeros_like(sums)
    for block in range(mixed.shape[0] // BLOCK):
        low, high = key_start(block), (block + 1) * BLOCK
        rows = slice(block * BLOCK, high)
        distance = masked_distance(seg_col, seg_row, block)
        for head in range(2):
            at = head * 3 * HEAD_DIM
            query = mixed[rows, at : at + HEAD_DIM] * BF(HEAD_DIM**-0.5)
            keys = mixed[low:high, at + HEAD_DIM : at + 2 * HEAD_DIM]
            values = mixed[low:high, at + 2 * HEAD_DIM : at + 3 * HEAD_DIM]
            grad = grad_context[rows, head * HEAD_DIM : (head + 1) * HEAD_DIM]
            scores = dot_nt(query, keys) - slope_of(base + head) * distance
            weights = jnp.exp(scores - logsum[0, rows, head : head + 1])
            grad_weights = dot_nt(grad, values)
            inner = jnp.sum(weights * grad_weights, axis=1, keepdims=True)
            grad_scores = (weights * (grad_weights - inner)).astype(BF)
            sums[head, 0, rows, :] = dot(grad_scores, keys) * HEAD_DIM**-0.5
            sums[head, 1, low:high, :] += dot_tn(grad_scores, query)
            sums[head, 2, low:high, :] += dot_tn(weights.astype(BF), grad)
    grad_mixed[...] = jnp.concatenate(
        [sums[head, kind] for head in range(2) for kind in range(3)], 1
    ).astype(BF)


def attention_specs(count):
    return [
        pl.BlockSpec((count, PAIR), lambda i: (0, i)),
        pl.BlockSpec((count, 1), lambda i: (0, 0)),
        pl.BlockSpec((1, count), lambda i: (0, 0)),
    ]


def attend_forward(mixed, seg_col, seg_row):
    count, width = mixed.shape
    pairs = width // PAIR
    return pl.pallas_call(
        functools.partial(forward_kernel, 2 * pairs),
        grid=(pairs,),
        in_specs=attention_specs(count),
        out_specs=[
            pl.BlockSpec((count, 2 * HEAD_DIM), lambda i: (0, i)),
            pl.BlockSpec((1, count, 2), lambda i: (i, 0, 0)),
        ],
        out_shape=[
            jax.ShapeDtypeStruct((count, pairs * 2 * HEAD_DIM), BF),
            jax.ShapeDtypeStruct((pairs, count, 2), F32),
        ],
        compiler_params=pltpu.CompilerParams(vmem_limit_bytes=32 * 2**20),
    )(mixed, seg_col, seg_row)


def attend_backward(mixed, seg_col, seg_row, logsum, grad_context):
    count, width = mixed.shape
    pairs = width // PAIR
    return pl.pallas_call(
        functools.partial(backward_kernel, 2 * pairs),
        grid=(pairs,),
        in_specs=attention_specs(count)
        + [
            pl.BlockSpec((1, count, 2), lambda i: (i, 0, 0)),
            pl.BlockSpec((count, 2 * HEAD_DIM), lambda i: (0, i)),
        ],
        out_specs=pl.BlockSpec((count, PAIR), lambda i: (0, i)),
        out_shape=jax.ShapeDtypeStruct((count, width), BF),
        scratch_shapes=[pltpu.VMEM((2, 3, count, HEAD_DIM), F32)],
        compiler_params=pltpu.CompilerParams(vmem_limit_bytes=32 * 2**20),
    )(mixed, seg_col, seg_row, logsum, grad_context)


def normalize(own, other):
    width = own.shape[1] + other.shape[1]
    center = (jnp.sum(own, axis=1) + jnp.sum(other, axis=1)) / width
    square = (jnp.sum(own * own, axis=1) + jnp.sum(other * other, axis=1)) / width
    scaled = lax.rsqrt(square - center * center + EPSILON)[:, None]
    return ((own - center[:, None]) * scaled, (other - center[:, None]) * scaled, scaled)


def shards(
    tokens,
    lengths,
    ln1_gain,
    ln1_shift,
    w_qkv,
    b_qv,
    w_out,
    b_out,
    ln2_gain,
    ln2_shift,
    w_up,
    b_up,
    w_down,
    b_down,
    cotangent,
):
    row = lax.axis_index("row")
    col = lax.axis_index("col")
    count = tokens.shape[0]
    model = 4 * tokens.shape[1]
    ends = jnp.cumsum(lengths[0])
    places = jnp.arange(count, dtype=jnp.int32)
    segment = jnp.sum((places[:, None] >= ends[None, :]).astype(jnp.int32), axis=1)
    seg_col, seg_row = segment[:, None], segment[None, :]

    def spread(block):
        mine = part(block, row, 0)
        crossed = swap_row(part(block, 1 - row, 0))
        theirs = swap_col(jnp.concatenate([mine, crossed], 1))
        width = mine.shape[1]
        own = in_order(col, mine, theirs[:, :width], 1)
        other = in_order(col, crossed, theirs[:, width:], 1)
        return own, other

    vectors = jnp.stack([ln1_gain, ln1_shift, ln2_gain, ln2_shift, b_out])
    crossed = swap_row(vectors)
    theirs = swap_col(jnp.concatenate([vectors, crossed], 1))
    quarter = vectors.shape[1]
    v_own = in_order(col, vectors, theirs[:, :quarter], 1)
    v_other = in_order(col, crossed, theirs[:, quarter:], 1)

    tok_own, tok_other = spread(tokens)
    w_qkv_o = swap_row(w_qkv)
    w_out_o = swap_row(w_out)
    w_up_o = swap_row(w_up)
    w_down_o = swap_row(w_down)
    cot_own, cot_other = spread(cotangent)

    x_own, x_other = tok_own.astype(F32), tok_other.astype(F32)
    u1_own, u1_other, r1 = normalize(x_own, x_other)
    n1_own = (u1_own * v_own[0] + v_own[1]).astype(BF)
    n1_other = (u1_other * v_other[0] + v_other[1]).astype(BF)
    pair_bias = b_qv.reshape(-1, 2, HEAD_DIM)
    joined_bias = jnp.stack(
        [pair_bias[:, 0], jnp.zeros_like(pair_bias[:, 0]), pair_bias[:, 1]], axis=1
    ).reshape(-1)
    mixed = (dot(n1_own, w_qkv) + dot(n1_other, w_qkv_o) + joined_bias).astype(BF)

    def to_heads(values):
        return in_order(row, part(values, row, 1), swap_row(part(values, 1 - row, 1)), 0)

    def to_tokens(values):
        return in_order(row, part(values, row, 0), swap_row(part(values, 1 - row, 0)), 1)

    head_mixed = to_heads(mixed)
    head_context, logsum = attend_forward(head_mixed, seg_col, seg_row)
    context = to_tokens(head_context)
    out_own = dot(context, w_out)
    got_own = swap_col(out_own.astype(BF))
    out_other = dot(context, w_out_o)
    got_other = swap_col(out_other.astype(BF))
    after_own = x_own + (out_own + got_own.astype(F32)) + v_own[4]
    after_other = x_other + (out_other + got_other.astype(F32)) + v_other[4]
    u2_own, u2_other, r2 = normalize(after_own, after_other)
    n2_own = (u2_own * v_own[2] + v_own[3]).astype(BF)
    n2_other = (u2_other * v_other[2] + v_other[3]).astype(BF)
    preact = dot(n2_own, w_up) + dot(n2_other, w_up_o) + b_up
    active = jax.nn.gelu(preact, approximate=True).astype(BF)

    grad_active = dot_nt(cot_own, w_down) + dot_nt(cot_other, w_down_o)
    unused, gelu_pull = jax.vjp(lambda values: jax.nn.gelu(values, approximate=True), preact)
    grad_pre = gelu_pull(grad_active)[0].astype(BF)
    gn_own = dot_nt(grad_pre, w_up)
    gn_got_own = swap_col(gn_own.astype(BF))
    gn_other = dot_nt(grad_pre, w_up_o)
    gn_got_other = swap_col(gn_other.astype(BF))

    def row_sum(own, other):
        return (own + swap_row(other.astype(BF)).astype(F32)).astype(BF)

    down_own, down_other = dot(active, w_down), dot(active, w_down_o)
    grad_w_down = row_sum(dot_tn(active, cot_own), dot_tn(active, cot_other))
    grad_w_up = row_sum(dot_tn(n2_own, grad_pre), dot_tn(n2_other, grad_pre))
    gain2_own = v_own[2] + nothing(grad_w_down)
    gain2_other = v_other[2] + nothing(grad_w_up)
    grad_w_down, grad_w_up = lax.psum((grad_w_down, grad_w_up), "dp")

    sent = jnp.concatenate([part(down_own, 1 - col, 1), part(down_other, 1 - col, 1)], 1)
    got = swap_col(sent.astype(BF)).astype(F32)
    res_own = part(after_own, col, 1) + part(down_own, col, 1) + got[:, :quarter]
    res_other = part(after_other, col, 1) + part(down_other, col, 1) + got[:, quarter:]
    block_out = (in_order(row, res_own, swap_row(res_other.astype(BF)).astype(F32), 0) + b_down).astype(BF)

    gn_own = gn_own + gn_got_own.astype(F32)
    gn_other = gn_other + gn_got_other.astype(F32)
    e_own, e_other = gn_own * gain2_own, gn_other * gain2_other
    mean_e = (jnp.sum(e_own, axis=1) + jnp.sum(e_other, axis=1))[:, None] / model
    mean_eu = (jnp.sum(e_own * u2_own, axis=1) + jnp.sum(e_other * u2_other, axis=1))[:, None] / model
    ga_own = cot_own.astype(F32) + r2 * (e_own - mean_e - u2_own * mean_eu)
    ga_other = cot_other.astype(F32) + r2 * (e_other - mean_e - u2_other * mean_eu)
    low_own, low_other = ga_own.astype(BF), ga_other.astype(BF)
    grad_context = (dot_nt(low_own, w_out) + dot_nt(low_other, w_out_o)).astype(BF)
    head_grad = attend_backward(head_mixed, seg_col, seg_row, logsum, to_heads(grad_context))
    grad_w_out = row_sum(dot_tn(context, low_own), dot_tn(context, low_other))
    grad_mixed = to_tokens(head_grad)

    g1_own, g1_other = dot_nt(grad_mixed, w_qkv), dot_nt(grad_mixed, w_qkv_o)
    sent = jnp.concatenate([part(g1_own, 1 - col, 1), part(g1_other, 1 - col, 1)], 1)
    got = swap_col(sent.astype(BF)).astype(F32)
    e_own, e_other = g1_own * v_own[0], g1_other * v_other[0]
    sums = jnp.stack(
        [
            jnp.sum(e_own, axis=1) + jnp.sum(e_other, axis=1),
            jnp.sum(e_own * u1_own, axis=1) + jnp.sum(e_other * u1_other, axis=1),
        ]
    )
    sums = (sums + swap_col(sums)) / model
    mean_e, mean_eu = sums[0][:, None], sums[1][:, None]
    g1_own = part(g1_own, col, 1) + got[:, :quarter]
    g1_other = part(g1_other, col, 1) + got[:, quarter:]
    u1_own, u1_other = part(u1_own, col, 1), part(u1_other, col, 1)
    gi_own = part(ga_own, col, 1) + r1 * (
        g1_own * ln1_gain - mean_e - u1_own * mean_eu
    )
    gi_other = part(ga_other, col, 1) + r1 * (
        g1_other * part(v_other[0], col, 0) - mean_e - u1_other * mean_eu
    )
    grad_input = in_order(row, gi_own, swap_row(gi_other), 0)

    def columns(grad, unit):
        return [jnp.sum(part(grad * unit, col, 1), axis=0), jnp.sum(part(grad, col, 1), axis=0)]

    mixed_sums = jnp.sum(grad_mixed, axis=0, dtype=F32).reshape(-1, 3, HEAD_DIM)
    qv_sums = jnp.stack([mixed_sums[:, 0], mixed_sums[:, 2]], axis=1).reshape(-1)
    up_sums = jnp.sum(grad_pre, axis=0, dtype=F32)
    here = columns(gn_own, u2_own) + [jnp.sum(part(ga_own, col, 1), axis=0), qv_sums, up_sums]
    there = columns(gn_other, u2_other) + [jnp.sum(part(ga_other, col, 1), axis=0), qv_sums, up_sums]
    here += [jnp.sum(g1_own * u1_own, axis=0), jnp.sum(g1_own, axis=0)]
    there += [jnp.sum(g1_other * u1_other, axis=0), jnp.sum(g1_other, axis=0)]
    small = jnp.concatenate(here) + swap_row(jnp.concatenate(there))
    small = jnp.concatenate([small, jnp.sum(cotangent, axis=0, dtype=F32)])
    small = small_sum(small.reshape(-1, 128)).reshape(-1)
    grad_w_qkv = row_sum(dot_tn(n1_own, grad_mixed), dot_tn(n1_other, grad_mixed))
    width = grad_w_out.shape[1]
    pieces = [grad_w_qkv[:, at : at + width] for at in range(0, grad_w_qkv.shape[1], width)]
    joined = ring_sum(jnp.concatenate(pieces + [grad_w_out], 0)).astype(F32)
    rows = grad_w_qkv.shape[0]
    grad_w_qkv = jnp.concatenate([joined[at * rows : (at + 1) * rows] for at in range(len(pieces))], 1)
    grad_w_out = joined[len(pieces) * rows :]
    cuts = [0]
    for size in (quarter, quarter, quarter, b_qv.shape[0], b_up.shape[0], quarter, quarter, quarter):
        cuts.append(cuts[-1] + size)
    g_ln2_gain, g_ln2_shift, g_b_out, g_b_qv, g_b_up, g_ln1_gain, g_ln1_shift, g_b_down = [
        small[a:b] for a, b in zip(cuts[:-1], cuts[1:])
    ]
    return (
        block_out,
        grad_input,
        g_ln1_gain,
        g_ln1_shift,
        grad_w_qkv,
        g_b_qv,
        grad_w_out,
        g_b_out,
        g_ln2_gain,
        g_ln2_shift,
        grad_w_up.astype(F32),
        g_b_up,
        grad_w_down.astype(F32),
        g_b_down,
    )


def solution(mesh):
    vector = P(("row", "col"))
    in_specs = (
        P("dp", ("row", "col")),
        P("dp", None),
        vector,
        vector,
        P("row", "col"),
        P("col"),
        P("col", "row"),
        vector,
        vector,
        vector,
        P("row", "col"),
        P("col"),
        P("col", "row"),
        vector,
        P("dp", ("row", "col")),
    )
    out_specs = (
        P("dp", ("row", "col")),
        P("dp", ("row", "col")),
        vector,
        vector,
        P("row", "col"),
        P("col"),
        P("col", "row"),
        vector,
        vector,
        vector,
        P("row", "col"),
        P("col"),
        P("col", "row"),
        vector,
    )
    return jax.shard_map(shards, mesh=mesh, in_specs=in_specs, out_specs=out_specs, check_vma=False)
```

```python
import functools

import jax
import jax.numpy as jnp
from jax import lax
from jax.experimental import pallas as pl
from jax.experimental.pallas import tpu as pltpu
from jax.sharding import PartitionSpec as P

HEADS = 16
HEAD_DIM = 64
MAXLEN = 512
BLOCK = 256
PAIR = 6 * HEAD_DIM
EPSILON = 1e-05
FAR = 1e12
BF = jnp.bfloat16
F32 = jnp.float32


def swap_row(values):
    return lax.ppermute(values, "row", [(0, 1), (1, 0)])


def swap_col(values):
    return lax.ppermute(values, "col", [(0, 1), (1, 0)])


def ring_sum(values):
    size = lax.axis_size("dp")
    if size == 1:
        return values
    places = list(range(0, size, 2)) + list(range(size - 1, 0, -2))
    forward = [(places[i], places[(i + 1) % size]) for i in range(size)]
    backward = [(to, start) for start, to in forward]
    place = jnp.array([places.index(i) for i in range(size)], jnp.int32)[lax.axis_index("dp")]
    rows = values.shape[0] // (2 * size)
    result = jnp.zeros(values.shape, values.dtype)
    held = [None, None]
    for step in range(2 * size - 1):
        for way, (perm, sign) in enumerate(((forward, 1), (backward, -1))):
            chunk = (place - sign * step) % size
            offset = (way * size + chunk) * rows
            if step == 0:
                held[way] = lax.dynamic_slice_in_dim(values, offset, rows, 0)
                continue
            held[way] = lax.ppermute(held[way], "dp", perm)
            if step < size:
                held[way] = held[way] + lax.dynamic_slice_in_dim(values, offset, rows, 0)
            if step >= size - 1:
                result = lax.dynamic_update_slice_in_dim(result, held[way], offset, 0)
    return result


def small_sum(values):
    size = lax.axis_size("dp")
    if size & (size - 1):
        return lax.psum(values, "dp")
    bit = 1
    while bit < size:
        values = values + lax.ppermute(values, "dp", [(i, i ^ bit) for i in range(size)])
        bit *= 2
    return values


def nothing(values):
    return values[0, 0].astype(F32) * 0.0


def part(values, index, axis):
    width = values.shape[axis] // 2
    return lax.dynamic_slice_in_dim(values, index * width, width, axis)


def in_order(index, mine, theirs, axis):
    first = jnp.where(index == 0, mine, theirs)
    second = jnp.where(index == 0, theirs, mine)
    return jnp.concatenate([first, second], axis)


def dot(a, b):
    return lax.dot_general(a, b, (((1,), (0,)), ((), ())), preferred_element_type=F32)


def dot_nt(a, b):
    return lax.dot_general(a, b, (((1,), (1,)), ((), ())), preferred_element_type=F32)


def dot_tn(a, b):
    return lax.dot_general(a, b, (((0,), (0,)), ((), ())), preferred_element_type=F32)


def key_start(block):
    return max(0, block * BLOCK - -(-(MAXLEN - 1) // BLOCK) * BLOCK)


def masked_distance(seg_col, seg_row, block):
    low, high = key_start(block), (block + 1) * BLOCK
    rows = slice(block * BLOCK, high)
    query = block * BLOCK + lax.broadcasted_iota(jnp.int32, (BLOCK, high - low), 0)
    key = low + lax.broadcasted_iota(jnp.int32, (BLOCK, high - low), 1)
    allowed = (seg_col[rows, :] == seg_row[:, low:high]) & (key <= query)
    return jnp.where(allowed, (query - key).astype(F32), FAR)


def slope_of(head):
    return jnp.exp2(-8.0 * (jnp.full((1, 1), head, jnp.int32).astype(F32) + 1.0) / HEADS)


def first_head(step, heads):
    return (lax.axis_index("col") * 2 + lax.axis_index("row")) * heads + 2 * step


def forward_kernel(heads, mixed, seg_col, seg_row, context, logsum):
    base = first_head(pl.program_id(0), heads)
    for block in range(mixed.shape[0] // BLOCK):
        low, high = key_start(block), (block + 1) * BLOCK
        rows = slice(block * BLOCK, high)
        distance = masked_distance(seg_col, seg_row, block)
        outs, logs = [], []
        for head in range(2):
            at = head * 3 * HEAD_DIM
            query = mixed[rows, at : at + HEAD_DIM] * BF(HEAD_DIM**-0.5)
            keys = mixed[low:high, at + HEAD_DIM : at + 2 * HEAD_DIM]
            values = mixed[low:high, at + 2 * HEAD_DIM : at + 3 * HEAD_DIM]
            scores = dot_nt(query, keys) - slope_of(base + head) * distance
            ceiling = jnp.max(scores, axis=1, keepdims=True)
            weights = jnp.exp(scores - ceiling)
            total = jnp.sum(weights, axis=1, keepdims=True)
            outs.append(dot(weights.astype(BF), values) / total)
            logs.append(ceiling + jnp.log(total))
        context[rows, :] = jnp.concatenate(outs, 1).astype(BF)
        logsum[0, rows, :] = jnp.concatenate(logs, 1)


def backward_kernel(heads, mixed, seg_col, seg_row, logsum, grad_context, grad_mixed, sums):
    base = first_head(pl.program_id(0), heads)
    sums[...] = jnp.zeros_like(sums)
    for block in range(mixed.shape[0] // BLOCK):
        low, high = key_start(block), (block + 1) * BLOCK
        rows = slice(block * BLOCK, high)
        distance = masked_distance(seg_col, seg_row, block)
        for head in range(2):
            at = head * 3 * HEAD_DIM
            query = mixed[rows, at : at + HEAD_DIM] * BF(HEAD_DIM**-0.5)
            keys = mixed[low:high, at + HEAD_DIM : at + 2 * HEAD_DIM]
            values = mixed[low:high, at + 2 * HEAD_DIM : at + 3 * HEAD_DIM]
            grad = grad_context[rows, head * HEAD_DIM : (head + 1) * HEAD_DIM]
            scores = dot_nt(query, keys) - slope_of(base + head) * distance
            weights = jnp.exp(scores - logsum[0, rows, head : head + 1])
            grad_weights = dot_nt(grad, values)
            inner = jnp.sum(weights * grad_weights, axis=1, keepdims=True)
            grad_scores = (weights * (grad_weights - inner)).astype(BF)
            sums[head, 0, rows, :] = dot(grad_scores, keys) * HEAD_DIM**-0.5
            sums[head, 1, low:high, :] += dot_tn(grad_scores, query)
            sums[head, 2, low:high, :] += dot_tn(weights.astype(BF), grad)
    grad_mixed[...] = jnp.concatenate(
        [sums[head, kind] for head in range(2) for kind in range(3)], 1
    ).astype(BF)


def attention_specs(count):
    return [
        pl.BlockSpec((count, PAIR), lambda i: (0, i)),
        pl.BlockSpec((count, 1), lambda i: (0, 0)),
        pl.BlockSpec((1, count), lambda i: (0, 0)),
    ]


def attend_forward(mixed, seg_col, seg_row):
    count, width = mixed.shape
    pairs = width // PAIR
    return pl.pallas_call(
        functools.partial(forward_kernel, 2 * pairs),
        grid=(pairs,),
        in_specs=attention_specs(count),
        out_specs=[
            pl.BlockSpec((count, 2 * HEAD_DIM), lambda i: (0, i)),
            pl.BlockSpec((1, count, 2), lambda i: (i, 0, 0)),
        ],
        out_shape=[
            jax.ShapeDtypeStruct((count, pairs * 2 * HEAD_DIM), BF),
            jax.ShapeDtypeStruct((pairs, count, 2), F32),
        ],
        compiler_params=pltpu.CompilerParams(vmem_limit_bytes=32 * 2**20),
    )(mixed, seg_col, seg_row)


def attend_backward(mixed, seg_col, seg_row, logsum, grad_context):
    count, width = mixed.shape
    pairs = width // PAIR
    return pl.pallas_call(
        functools.partial(backward_kernel, 2 * pairs),
        grid=(pairs,),
        in_specs=attention_specs(count)
        + [
            pl.BlockSpec((1, count, 2), lambda i: (i, 0, 0)),
            pl.BlockSpec((count, 2 * HEAD_DIM), lambda i: (0, i)),
        ],
        out_specs=pl.BlockSpec((count, PAIR), lambda i: (0, i)),
        out_shape=jax.ShapeDtypeStruct((count, width), BF),
        scratch_shapes=[pltpu.VMEM((2, 3, count, HEAD_DIM), F32)],
        compiler_params=pltpu.CompilerParams(vmem_limit_bytes=32 * 2**20),
    )(mixed, seg_col, seg_row, logsum, grad_context)


def normalize(own, other):
    width = own.shape[1] + other.shape[1]
    center = (jnp.sum(own, axis=1) + jnp.sum(other, axis=1)) / width
    square = (jnp.sum(own * own, axis=1) + jnp.sum(other * other, axis=1)) / width
    scaled = lax.rsqrt(square - center * center + EPSILON)[:, None]
    return ((own - center[:, None]) * scaled, (other - center[:, None]) * scaled, scaled)


def shards(
    tokens,
    lengths,
    ln1_gain,
    ln1_shift,
    w_qkv,
    b_qv,
    w_out,
    b_out,
    ln2_gain,
    ln2_shift,
    w_up,
    b_up,
    w_down,
    b_down,
    cotangent,
):
    row = lax.axis_index("row")
    col = lax.axis_index("col")
    count = tokens.shape[0]
    model = 4 * tokens.shape[1]
    ends = jnp.cumsum(lengths[0])
    places = jnp.arange(count, dtype=jnp.int32)
    segment = jnp.sum((places[:, None] >= ends[None, :]).astype(jnp.int32), axis=1)
    seg_col, seg_row = segment[:, None], segment[None, :]

    def spread(block):
        mine = part(block, row, 0)
        crossed = swap_row(part(block, 1 - row, 0))
        theirs = swap_col(jnp.concatenate([mine, crossed], 1))
        width = mine.shape[1]
        own = in_order(col, mine, theirs[:, :width], 1)
        other = in_order(col, crossed, theirs[:, width:], 1)
        return own, other

    vectors = jnp.stack([ln1_gain, ln1_shift, ln2_gain, ln2_shift, b_out])
    crossed = swap_row(vectors)
    theirs = swap_col(jnp.concatenate([vectors, crossed], 1))
    quarter = vectors.shape[1]
    v_own = in_order(col, vectors, theirs[:, :quarter], 1)
    v_other = in_order(col, crossed, theirs[:, quarter:], 1)

    tok_own, tok_other = spread(tokens)
    w_qkv_o = swap_row(w_qkv)
    w_out_o = swap_row(w_out)
    w_up_o = swap_row(w_up)
    w_down_o = swap_row(w_down)
    cot_own, cot_other = spread(cotangent)

    x_own, x_other = tok_own.astype(F32), tok_other.astype(F32)
    u1_own, u1_other, r1 = normalize(x_own, x_other)
    n1_own = (u1_own * v_own[0] + v_own[1]).astype(BF)
    n1_other = (u1_other * v_other[0] + v_other[1]).astype(BF)
    pair_bias = b_qv.reshape(-1, 2, HEAD_DIM)
    joined_bias = jnp.stack(
        [pair_bias[:, 0], jnp.zeros_like(pair_bias[:, 0]), pair_bias[:, 1]], axis=1
    ).reshape(-1)
    mixed = (dot(n1_own, w_qkv) + dot(n1_other, w_qkv_o) + joined_bias).astype(BF)

    def to_heads(values):
        return in_order(row, part(values, row, 1), swap_row(part(values, 1 - row, 1)), 0)

    def to_tokens(values):
        return in_order(row, part(values, row, 0), swap_row(part(values, 1 - row, 0)), 1)

    head_mixed = to_heads(mixed)
    head_context, logsum = attend_forward(head_mixed, seg_col, seg_row)
    context = to_tokens(head_context)
    out_own = dot(context, w_out)
    got_own = swap_col(out_own.astype(BF))
    out_other = dot(context, w_out_o)
    got_other = swap_col(out_other.astype(BF))
    after_own = x_own + (out_own + got_own.astype(F32)) + v_own[4]
    after_other = x_other + (out_other + got_other.astype(F32)) + v_other[4]
    u2_own, u2_other, r2 = normalize(after_own, after_other)
    n2_own = (u2_own * v_own[2] + v_own[3]).astype(BF)
    n2_other = (u2_other * v_other[2] + v_other[3]).astype(BF)
    preact = dot(n2_own, w_up) + dot(n2_other, w_up_o) + b_up
    active = jax.nn.gelu(preact, approximate=True).astype(BF)

    grad_active = dot_nt(cot_own, w_down) + dot_nt(cot_other, w_down_o)
    unused, gelu_pull = jax.vjp(lambda values: jax.nn.gelu(values, approximate=True), preact)
    grad_pre = gelu_pull(grad_active)[0].astype(BF)
    gn_own = dot_nt(grad_pre, w_up)
    gn_got_own = swap_col(gn_own.astype(BF))
    gn_other = dot_nt(grad_pre, w_up_o)
    gn_got_other = swap_col(gn_other.astype(BF))

    def row_sum(own, other):
        return (own + swap_row(other.astype(BF)).astype(F32)).astype(BF)

    down_own, down_other = dot(active, w_down), dot(active, w_down_o)
    grad_w_down = row_sum(dot_tn(active, cot_own), dot_tn(active, cot_other))
    grad_w_up = row_sum(dot_tn(n2_own, grad_pre), dot_tn(n2_other, grad_pre))
    gain2_own = v_own[2] + nothing(grad_w_down)
    gain2_other = v_other[2] + nothing(grad_w_up)
    grad_w_up = lax.psum(grad_w_up, "dp")
    grad_w_down = ring_sum(grad_w_down)

    sent = jnp.concatenate([part(down_own, 1 - col, 1), part(down_other, 1 - col, 1)], 1)
    got = swap_col(sent.astype(BF)).astype(F32)
    res_own = part(after_own, col, 1) + part(down_own, col, 1) + got[:, :quarter]
    res_other = part(after_other, col, 1) + part(down_other, col, 1) + got[:, quarter:]
    block_out = (in_order(row, res_own, swap_row(res_other.astype(BF)).astype(F32), 0) + b_down).astype(BF)

    gn_own = gn_own + gn_got_own.astype(F32)
    gn_other = gn_other + gn_got_other.astype(F32)
    e_own, e_other = gn_own * gain2_own, gn_other * gain2_other
    mean_e = (jnp.sum(e_own, axis=1) + jnp.sum(e_other, axis=1))[:, None] / model
    mean_eu = (jnp.sum(e_own * u2_own, axis=1) + jnp.sum(e_other * u2_other, axis=1))[:, None] / model
    ga_own = cot_own.astype(F32) + r2 * (e_own - mean_e - u2_own * mean_eu)
    ga_other = cot_other.astype(F32) + r2 * (e_other - mean_e - u2_other * mean_eu)
    low_own, low_other = ga_own.astype(BF), ga_other.astype(BF)
    grad_context = (dot_nt(low_own, w_out) + dot_nt(low_other, w_out_o)).astype(BF)
    head_grad = attend_backward(head_mixed, seg_col, seg_row, logsum, to_heads(grad_context))
    grad_w_out = row_sum(dot_tn(context, low_own), dot_tn(context, low_other))
    grad_mixed = to_tokens(head_grad)

    g1_own, g1_other = dot_nt(grad_mixed, w_qkv), dot_nt(grad_mixed, w_qkv_o)
    sent = jnp.concatenate([part(g1_own, 1 - col, 1), part(g1_other, 1 - col, 1)], 1)
    got = swap_col(sent.astype(BF)).astype(F32)
    e_own, e_other = g1_own * v_own[0], g1_other * v_other[0]
    sums = jnp.stack(
        [
            jnp.sum(e_own, axis=1) + jnp.sum(e_other, axis=1),
            jnp.sum(e_own * u1_own, axis=1) + jnp.sum(e_other * u1_other, axis=1),
        ]
    )
    sums = (sums + swap_col(sums)) / model
    mean_e, mean_eu = sums[0][:, None], sums[1][:, None]
    g1_own = part(g1_own, col, 1) + got[:, :quarter]
    g1_other = part(g1_other, col, 1) + got[:, quarter:]
    u1_own, u1_other = part(u1_own, col, 1), part(u1_other, col, 1)
    gi_own = part(ga_own, col, 1) + r1 * (
        g1_own * ln1_gain - mean_e - u1_own * mean_eu
    )
    gi_other = part(ga_other, col, 1) + r1 * (
        g1_other * part(v_other[0], col, 0) - mean_e - u1_other * mean_eu
    )
    grad_input = in_order(row, gi_own, swap_row(gi_other), 0)

    def columns(grad, unit):
        return [jnp.sum(part(grad * unit, col, 1), axis=0), jnp.sum(part(grad, col, 1), axis=0)]

    mixed_sums = jnp.sum(grad_mixed, axis=0, dtype=F32).reshape(-1, 3, HEAD_DIM)
    qv_sums = jnp.stack([mixed_sums[:, 0], mixed_sums[:, 2]], axis=1).reshape(-1)
    up_sums = jnp.sum(grad_pre, axis=0, dtype=F32)
    here = columns(gn_own, u2_own) + [jnp.sum(part(ga_own, col, 1), axis=0), qv_sums, up_sums]
    there = columns(gn_other, u2_other) + [jnp.sum(part(ga_other, col, 1), axis=0), qv_sums, up_sums]
    here += [jnp.sum(g1_own * u1_own, axis=0), jnp.sum(g1_own, axis=0)]
    there += [jnp.sum(g1_other * u1_other, axis=0), jnp.sum(g1_other, axis=0)]
    small = jnp.concatenate(here) + swap_row(jnp.concatenate(there))
    small = jnp.concatenate([small, jnp.sum(cotangent, axis=0, dtype=F32)])
    small = small_sum(small.reshape(-1, 128)).reshape(-1)
    grad_w_qkv = row_sum(dot_tn(n1_own, grad_mixed), dot_tn(n1_other, grad_mixed))
    width = grad_w_out.shape[1]
    pieces = [grad_w_qkv[:, at : at + width] for at in range(0, grad_w_qkv.shape[1], width)]
    pieces[0] = pieces[0] + nothing(grad_w_down).astype(BF)
    joined = ring_sum(jnp.concatenate(pieces + [grad_w_out], 0)).astype(F32)
    grad_w_up = grad_w_up.astype(F32) + nothing(joined)
    rows = grad_w_qkv.shape[0]
    grad_w_qkv = jnp.concatenate([joined[at * rows : (at + 1) * rows] for at in range(len(pieces))], 1)
    grad_w_out = joined[len(pieces) * rows :]
    cuts = [0]
    for size in (quarter, quarter, quarter, b_qv.shape[0], b_up.shape[0], quarter, quarter, quarter):
        cuts.append(cuts[-1] + size)
    g_ln2_gain, g_ln2_shift, g_b_out, g_b_qv, g_b_up, g_ln1_gain, g_ln1_shift, g_b_down = [
        small[a:b] for a, b in zip(cuts[:-1], cuts[1:])
    ]
    return (
        block_out,
        grad_input,
        g_ln1_gain,
        g_ln1_shift,
        grad_w_qkv,
        g_b_qv,
        grad_w_out,
        g_b_out,
        g_ln2_gain,
        g_ln2_shift,
        grad_w_up,
        g_b_up,
        grad_w_down.astype(F32),
        g_b_down,
    )


def solution(mesh):
    vector = P(("row", "col"))
    in_specs = (
        P("dp", ("row", "col")),
        P("dp", None),
        vector,
        vector,
        P("row", "col"),
        P("col"),
        P("col", "row"),
        vector,
        vector,
        vector,
        P("row", "col"),
        P("col"),
        P("col", "row"),
        vector,
        P("dp", ("row", "col")),
    )
    out_specs = (
        P("dp", ("row", "col")),
        P("dp", ("row", "col")),
        vector,
        vector,
        P("row", "col"),
        P("col"),
        P("col", "row"),
        vector,
        vector,
        vector,
        P("row", "col"),
        P("col"),
        P("col", "row"),
        vector,
    )
    return jax.shard_map(shards, mesh=mesh, in_specs=in_specs, out_specs=out_specs, check_vma=False)
```
